256 devices in a mesh: pair: 64 (over z, x, core), ri: 4 (over y).
Axes of the slice: x: 4, y: 4, z: 8, core: 2. Of those that a mesh axis runs over, the one named last changes fastest.
Arguments:
- tensor: bfloat16 [64, 3, 192, 128, 128], P('pair', None, 'ri'), may hold values from -0.875 to 0.875
- live: int32 [64, 3], replicated, may hold values 0 or 1
- sizes: int32 [64], replicated, may hold values from 64 to 128
- occ_density: bfloat16 [64, 3, 128, 128], P('pair', None, 'ri'), may hold values from -0.2066757 to 0.2066757, as said below
- vir_density: bfloat16 [64, 3, 128, 128], P('pair', None, 'ri'), may hold values from -0.2066757 to 0.2066757, as said below
Outputs:
- chi: float32 [64, 3, 192, 192], P('pair', None, None, 'ri')
The draws below stay inside these ranges and needn't reach their ends.
Inputs may be any that keep to these rules, and one draw needn't show every extreme that they name: `occ_density`: the blocks form a symmetric matrix: block (a, a+k) is the transpose of block (a+k, a), cluster indices modulo 64. `vir_density`: the blocks form a symmetric matrix: block (a, a+k) is the transpose of block (a+k, a), cluster indices modulo 64.
All inputs are finite; a program needn't handle non-finite values.
Results may differ from the reference program's by a relative error of at most 0.004.
Values may be sent and summed in bfloat16 or wider, within the bound.
A program may use at most 192 MiB of HBM per device.

```python
import jax
import jax.numpy as jnp
from jax import lax

BLK = 128
RBLK = 192
NB = 64


def banded_symmetric(key):
    key_list = jax.random.split(key, 2)
    dims_tuple = (NB, BLK, BLK)
    samples = [jax.random.normal(k, dims_tuple, jnp.float32) for k in key_list]
    diagonal = (samples[0] + jnp.swapaxes(samples[0], 1, 2)) * 0.7
    upper_block = samples[1]
    lower_block = jnp.swapaxes(jnp.roll(upper_block, 1, axis=0), 1, 2)
    stacked = jnp.stack([lower_block, diagonal, upper_block], axis=1)
    return (jnp.clip(stacked, -4.0, 4.0) * (3.0 * BLK) ** (-0.5)).astype(jnp.bfloat16)


def draw_occ_density(key, part):
    return banded_symmetric(jax.random.fold_in(key, 17))


def draw_vir_density(key, part):
    return banded_symmetric(jax.random.fold_in(key, 29))


def place_ends(result, stream_key, least, top_value):
    longest = result.shape.index(max(result.shape))
    spots = []
    for shift in (0, 1):
        where = [jax.random.randint(jax.random.fold_in(stream_key, axis), (), 0, length) for axis, length in enumerate(result.shape)]
        where[longest] = (where[longest] + shift) % result.shape[longest]
        spots.append(tuple(where))
    return result.at[spots[0]].set(least).at[spots[1]].set(top_value)


def block_levels(own_key, shape, cuts, low, high):
    level = 1.0
    for dim, parts in cuts:
        steps = jax.random.uniform(jax.random.fold_in(jax.random.fold_in(own_key, 6), dim), (parts,), jnp.float32, low / len(cuts), high / len(cuts))
        level = level * jnp.repeat(jnp.exp(steps), shape[dim] // parts).reshape((-1,) + (1,) * (len(shape) - 1 - dim))
    return level


def noise(key, dims, deviation, most, cuts=(), kind=jnp.bfloat16):
    gain = block_levels(key, dims, cuts, -0.22, 0.18) if cuts else 1.0
    values = jax.random.normal(key, dims, jnp.float32) * deviation * gain
    return jnp.minimum(jnp.maximum(values, -most), most).astype(kind)


def setup_inputs(seed: int = 0) -> dict:
    splits = jax.random.split(jax.random.key(seed), 6)
    return {
        "tensor": noise(splits[0], (NB, 3, RBLK, BLK, BLK), (1.6 * BLK ** -0.5), 0.875, ((0, 64), (2, 4))),
        "live": place_ends((jax.random.randint(splits[1], (NB, 3), 0, 4) < 3).astype(jnp.int32), jax.random.fold_in(splits[1], 1), 0, 1),
        "sizes": place_ends(jax.random.randint(splits[2], (NB,), BLK // 2, BLK + 1), jax.random.fold_in(splits[2], 1), BLK // 2, BLK).astype(jnp.int32),
        "occ_density": draw_occ_density(jax.random.fold_in(splits[5], 71), 0),
        "vir_density": draw_vir_density(jax.random.fold_in(splits[5], 71), 0),
    }


HIGH = lax.Precision.HIGHEST


def cluster_rows(tensor, live, sizes, cluster):
    lane_index = jnp.arange(BLK, dtype=jnp.int32)
    neighbours = jnp.mod(cluster + jnp.arange(-1, 2, dtype=jnp.int32), NB).astype(jnp.int32)
    nbr_sizes = jnp.take(sizes, neighbours)
    flags = lax.dynamic_index_in_dim(live, cluster, 0, keepdims=False)
    own_size = lax.dynamic_index_in_dim(sizes, cluster, 0, keepdims=False)
    keep_mask = (flags[:, None, None] > 0) & (lane_index[None, :, None] < own_size) & (lane_index[None, None, :] < nbr_sizes[:, None, None])
    block_rows = lax.dynamic_index_in_dim(tensor, cluster, 0, keepdims=False)
    return block_rows * keep_mask[:, None, :, :].astype(block_rows.dtype)


def reference(tensor, live, sizes, occ_density, vir_density):
    def one_cluster(cluster):
        own_rows = cluster_rows(tensor, live, sizes, cluster)
        own_flat = own_rows.reshape(3, RBLK, -1)
        occ_row = lax.dynamic_index_in_dim(occ_density, cluster, 0, keepdims=False).astype(jnp.float32)
        blocks = []
        for g in (-1, 0, 1):
            source = jnp.mod(cluster + g, NB).astype(jnp.int32)
            source_rows = cluster_rows(tensor, live, sizes, source).astype(jnp.float32)
            chi_block = jnp.zeros((RBLK, RBLK), jnp.float32)
            for u in (-1, 0, 1):
                t = u - g
                running = jnp.zeros((RBLK, BLK, BLK), jnp.float32)
                for s in (-1, 0, 1):
                    if abs(t - s) <= 1:
                        panel_index = jnp.mod(source + s, NB).astype(jnp.int32)
                        panel = lax.dynamic_index_in_dim(vir_density, panel_index, 0, keepdims=False)[t - s + 1].astype(jnp.float32)
                        running = running + jnp.einsum("pml,ls->pms", source_rows[s + 1], panel, precision=HIGH)
                half_rows = lax.optimization_barrier(running.astype(jnp.bfloat16)).astype(jnp.float32)
                near_rows = jnp.einsum("nm,pms->pns", occ_row[g + 1], half_rows, precision=HIGH)
                near_bf = lax.optimization_barrier(near_rows.astype(jnp.bfloat16))
                chi_block = chi_block + lax.dot_general(near_bf.reshape(RBLK, -1), own_flat[u + 1], (((1,), (1,)), ((), ())), preferred_element_type=jnp.float32)
            blocks.append(chi_block)
        return jnp.stack(blocks)

    return lax.map(one_cluster, jnp.arange(NB, dtype=jnp.int32))
```

```python
import functools

import jax
import jax.numpy as jnp
from jax import lax
from jax.experimental import pallas as pl
from jax.experimental.pallas import tpu as pltpu
from jax.sharding import PartitionSpec as P

MESH = pl.DeviceIdType.MESH
BF = jnp.bfloat16
F32 = jnp.float32
NT = (((1,), (1,)), ((), ()))
MC = 32
LAG = 2


def kernel(
    ncl, nri,
    ten, live, sizes, occ, vir,
    out,
    nat, fnat, own_t, up_t, c1a, c1b, cmb,
    z0, zp, zm, f0, fp, zn, perm, vmat, omat, occ_f, vir_f, acc, rin, rsend,
    s_nat, r_nat, l_nat, s_up, r_up, s_c1a, r_c1a, s_c1b, r_c1b, s_cmb, r_cmb,
    s_occ, r_occ, s_vir, r_vir, l_den, s_res, r_res,
):
    S = ten.shape[2]
    B = ten.shape[3]
    DR = occ.shape[2]
    NQ = S // 16
    NMC = B // MC
    NK = 3 * NMC
    c = lax.axis_index("pair")
    y = lax.axis_index("ri")

    def cl(d):
        return lax.rem(c + (d + ncl), ncl)

    def rw(d):
        return lax.rem(y + (d + nri), nri)

    def remote(src, dst, ss, rs, dc, dy):
        return pltpu.make_async_remote_copy(
            src_ref=src, dst_ref=dst, send_sem=ss, recv_sem=rs,
            device_id=(cl(dc), rw(dy)), device_id_type=MESH,
        )

    barrier = pltpu.get_barrier_semaphore()
    others = [(dc, dy) for dc in (-1, 0, 1) for dy in range(nri) if (dc, dy) != (0, 0)]
    for dc, dy in others:
        pl.semaphore_signal(barrier, inc=1, device_id=(cl(dc), rw(dy)), device_id_type=MESH)

    nat_copies = [
        pltpu.make_async_copy(ten.at[0, s], nat.at[s], l_nat.at[s]) for s in range(3)
    ]
    for cp in nat_copies:
        cp.start()
    my_rows = pl.ds(pl.multiple_of(y * DR, DR), DR)
    den_copies = [
        pltpu.make_async_copy(occ.at[0], occ_f.at[:, my_rows], l_den.at[0]),
        pltpu.make_async_copy(vir.at[0], vir_f.at[1, :, my_rows], l_den.at[1]),
    ]
    for cp in den_copies:
        cp.start()
    row = lax.broadcasted_iota(jnp.int32, (256, 256), 0)
    col = lax.broadcasted_iota(jnp.int32, (256, 256), 1)
    perm[...] = jnp.where(
        (row // 16 == col % 16) & (row % 16 == col // 16), 1.0, 0.0
    ).astype(BF)
    for r in range(acc.shape[0]):
        acc[r] = jnp.zeros(acc.shape[1:], F32)
    pl.semaphore_wait(barrier, len(others))

    occ_sends, vir_sends = [], []
    for dy in range(1, nri):
        occ_sends.append(
            remote(occ.at[0], occ_f.at[:, my_rows], s_occ.at[dy - 1], r_occ.at[dy - 1], 0, dy)
        )
    for i, (dc, dy) in enumerate(others):
        vir_sends.append(
            remote(vir.at[0], vir_f.at[1 - dc, :, my_rows], s_vir.at[i], r_vir.at[i], dc, dy)
        )
    for cp in occ_sends + vir_sends:
        cp.start()

    nat_sends = []
    for j in range(NQ):
        q = pl.ds(16 * j, 16)
        nat_sends.append(
            remote(ten.at[0, :, q], fnat.at[:, q], s_nat.at[j], r_nat.at[j], 0, 1)
        )
    for cp in nat_sends:
        cp.start()

    def part(k):
        return lax.div(k, NMC), pl.ds(pl.multiple_of(lax.rem(k, NMC) * MC, MC), MC)

    def up_send(k):
        s, m = part(k)
        return remote(own_t.at[s, m], up_t.at[s, m], s_up.at[k], r_up.at[k], 0, -1)

    def c1a_send(k):
        s, m = part(k)
        return remote(own_t.at[s, m], c1a.at[s, m], s_c1a.at[k], r_c1a.at[k], -1, 0)

    def c1b_send(k):
        s, m = part(k)
        return remote(up_t.at[s, m], c1b.at[s, m], s_c1b.at[k], r_c1b.at[k], -1, 0)

    def cmb_send(k):
        s, m = part(k)
        return remote(up_t.at[s, m], cmb.at[s, m], s_cmb.at[k], r_cmb.at[k], 1, 0)

    for s in range(3):
        nat_copies[s].wait()

        @pl.loop(0, NMC)
        def _(mc, s=s):
            for mb in range(MC // 16):
                m0 = pl.multiple_of(mc * MC + mb * 16, 16)
                for j in range(NQ):
                    x = nat[s, pl.ds(16 * j, 16), pl.ds(m0, 16), :].reshape(256, B)
                    t = jnp.dot(perm[...], x, preferred_element_type=F32).astype(BF)
                    own_t[s, pl.ds(m0, 16), pl.ds(16 * j, 16), :] = t.reshape(16, 16, B)
            k = s * NMC + mc
            up_send(k).start()
            c1a_send(k).start()

    for cp in den_copies:
        cp.wait()
    for cp in occ_sends + vir_sends:
        cp.wait_recv()
    size = {d: sizes[cl(d)] for d in range(-2, 3)}
    ri_ = lax.broadcasted_iota(jnp.int32, (B, B), 0)
    ci_ = lax.broadcasted_iota(jnp.int32, (B, B), 1)
    for u in (-1, 0, 1):
        on = live[c, u + 1].astype(F32)
        for t in (u - 1, u, u + 1):
            keep = jnp.where((ri_ < size[u]) & (ci_ < size[t]), on, 0.0)
            v = vir_f[u + 1, t - u + 1].astype(F32) * keep
            vmat[pl.ds((u + 1) * B, B), pl.ds((t + 2) * B, B)] = v.astype(BF)
    zero = jnp.zeros((B, B), BF)
    for u in (-1, 0, 1):
        for t in range(-2, 3):
            if abs(t - u) > 1:
                vmat[pl.ds((u + 1) * B, B), pl.ds((t + 2) * B, B)] = zero
    for g in (-1, 0, 1):
        o = occ_f[g + 1].astype(F32)
        o = jnp.where((ri_ < size[0]) & (ci_ < size[g]), o, 0.0)
        omat[g + 1] = o.T.astype(BF)

    def transform(src, q0, dests):
        @pl.loop(0, 8)
        def _(i):
            qs = [q0 + 2 * i, q0 + 2 * i + 1]
            x = jnp.concatenate(
                [jnp.concatenate([src[u, q] for u in range(3)], axis=1) for q in qs], axis=0
            )
            lo = jnp.dot(
                x[:, : 2 * B], vmat[pl.ds(0, 2 * B), pl.ds(0, 2 * B)],
                preferred_element_type=F32,
            ).astype(BF)
            mid = jnp.dot(
                x, vmat[:, pl.ds(2 * B, B)], preferred_element_type=F32
            ).astype(BF)
            hi = jnp.dot(
                x[:, B:], vmat[pl.ds(B, 2 * B), pl.ds(3 * B, 2 * B)],
                preferred_element_type=F32,
            ).astype(BF)
            yy = jnp.concatenate([lo, mid, hi], axis=1)
            for n in range(2):
                rows = yy[n * B : (n + 1) * B]
                for slot, (g, _dst) in enumerate(dests):
                    zn[slot, 2 * i + n] = jnp.dot(
                        omat[g + 1], rows[:, (g + 1) * B : (g + 4) * B],
                        preferred_element_type=F32,
                    ).astype(BF)

        @pl.loop(0, B // 16)
        def _(mb):
            m0 = pl.multiple_of(mb * 16, 16)
            for slot, (_g, dst) in enumerate(dests):
                x = zn[slot, :, pl.ds(m0, 16), :].reshape(256, 3 * B)
                t = jnp.dot(perm[...], x, preferred_element_type=F32).astype(BF)
                for s in range(3):
                    dst[s, pl.ds(m0, 16), pl.ds(q0, 16), :] = t[
                        :, s * B : (s + 1) * B
                    ].reshape(16, 16, B)

    @pl.loop(0, NQ)
    def _(j):
        transform(nat, pl.multiple_of(16 * j, 16), [(-1, zm), (0, z0), (1, zp)])

    def gram(r, left, right, dc, k):
        s, _ = part(k)
        m0 = lax.rem(k, NMC) * MC
        total = jnp.zeros((S, S), F32)
        for i in range(MC // 2):
            a = jnp.concatenate([left[s, m0 + 2 * i], left[s, m0 + 2 * i + 1]], axis=1)
            b = jnp.concatenate([right[s, m0 + 2 * i], right[s, m0 + 2 * i + 1]], axis=1)
            total += lax.dot_general(a, b, NT, preferred_element_type=F32)
        acc[r] += total * live[cl(dc), s].astype(F32)

    def late(k):
        c1b_send(k).wait_recv()
        gram(4, c1b, zp, 1, k)
        cmb_send(k).wait_recv()
        gram(6, cmb, zm, -1, k)

    cpj = NK // NQ

    @pl.loop(0, NQ)
    def _(j):
        @pl.loop(0, cpj)
        def _(kk):
            k = j * cpj + kk
            up_send(k).wait_recv()
            c1b_send(k).start()
            cmb_send(k).start()
            gram(0, own_t, z0, 0, k)
            gram(1, up_t, z0, 0, k)
            c1a_send(k).wait_recv()
            gram(3, c1a, zp, 1, k)

            @pl.when(k >= LAG)
            def _():
                late(k - LAG)

        q0 = pl.multiple_of(16 * j, 16)
        q = pl.ds(q0, 16)
        remote(ten.at[0, :, q], fnat.at[:, q], s_nat.at[j], r_nat.at[j], 0, 1).wait_recv()
        transform(fnat, q0, [(0, f0), (1, fp)])

    @pl.loop(NK - LAG, NK)
    def _(k):
        late(k)

    @pl.loop(0, NK)
    def _(k):
        gram(2, up_t, f0, 0, k)
        gram(5, c1b, fp, 1, k)

    routes = [
        (1, True, 0, 1),
        (2, True, 0, 1),
        (3, True, 1, 0),
        (4, True, 1, 1),
        (5, False, 0, -1),
        (5, True, 1, 1),
        (6, True, -1, 1),
    ]
    sends = []
    for i, (r, flip, dc, dy) in enumerate(routes):
        v = acc[r]
        rsend[i, :, pl.ds(0, S)] = v.T if flip else v
        cp = remote(rsend.at[i], rin.at[i], s_res.at[i], r_res.at[i], dc, dy)
        cp.start()
        sends.append(cp)

    def put(g, dy, v):
        out[g + 1, pl.ds(pl.multiple_of(rw(dy) * S, 16), S), :] = v

    put(0, 0, acc[0].T)
    put(0, 1, acc[1])
    put(1, 0, acc[3])
    put(1, 1, acc[4])
    put(-1, 1, acc[6])
    landed = [(0, -1), (0, -2), (-1, 0), (-1, -1), (1, 2), (-1, -2), (1, -1)]
    for i, (g, dy) in enumerate(landed):
        sends[i].wait_recv()
        put(g, dy, rin[i, :, pl.ds(0, S)])

    for cp in sends + occ_sends + vir_sends + nat_sends:
        cp.wait_send()

    @pl.loop(0, NK)
    def _(k):
        up_send(k).wait_send()
        c1a_send(k).wait_send()
        c1b_send(k).wait_send()
        cmb_send(k).wait_send()


def per_device(ncl, nri, tensor, live, sizes, occ, vir):
    S, B = tensor.shape[2], tensor.shape[3]
    NQ, NK = S // 16, 3 * (B // MC)
    block = pltpu.VMEM((3, B, S, B), BF)
    dma = lambda n: pltpu.SemaphoreType.DMA((n,))
    n_other = 3 * nri - 1
    any_, smem = pl.BlockSpec(memory_space=pl.ANY), pl.BlockSpec(memory_space=pltpu.SMEM)
    result = pl.pallas_call(
        functools.partial(kernel, ncl, nri),
        out_shape=jax.ShapeDtypeStruct((3, nri * S, S), F32),
        in_specs=[any_, smem, smem, any_, any_],
        out_specs=pl.BlockSpec(memory_space=pltpu.VMEM),
        scratch_shapes=[
            pltpu.VMEM((3, S, B, B), BF), pltpu.VMEM((3, S, B, B), BF),
            block, block, block, block, block,
            block, block, block, block, block,
            pltpu.VMEM((3, 16, B, 3 * B), BF),
            pltpu.VMEM((256, 256), BF),
            pltpu.VMEM((3 * B, 5 * B), BF),
            pltpu.VMEM((3, B, B), BF),
            pltpu.VMEM((3, B, B), BF),
            pltpu.VMEM((3, 3, B, B), BF),
            pltpu.VMEM((7, S, S), F32),
            pltpu.VMEM((7, S, 128), F32),
            pltpu.VMEM((7, S, 128), F32),
            dma(NQ), dma(NQ), dma(3),
            dma(NK), dma(NK), dma(NK), dma(NK), dma(NK), dma(NK), dma(NK), dma(NK),
            dma(nri - 1), dma(nri - 1), dma(n_other), dma(n_other), dma(2),
            dma(7), dma(7),
        ],
        compiler_params=pltpu.CompilerParams(
            collective_id=0, has_side_effects=True, vmem_limit_bytes=63 * 1024 * 1024
        ),
        name="polar",
    )(tensor, live, sizes, occ, vir)
    return result[None]


def solution(mesh):
    ncl, nri = mesh.shape["pair"], mesh.shape["ri"]
    in_specs = (
        P("pair", None, "ri", None, None),
        P(),
        P(),
        P("pair", None, "ri", None),
        P("pair", None, "ri", None),
    )
    return jax.shard_map(
        functools.partial(per_device, ncl, nri),
        mesh=mesh,
        in_specs=in_specs,
        out_specs=P("pair", None, None, "ri"),
        check_vma=False,
    )
```

```python
import functools

import jax
import jax.numpy as jnp
from jax import lax
from jax.experimental import pallas as pl
from jax.experimental.pallas import tpu as pltpu
from jax.sharding import PartitionSpec as P

MESH = pl.DeviceIdType.MESH
BF = jnp.bfloat16
F32 = jnp.float32
NT = (((1,), (1,)), ((), ()))
MC = 32
LAG = 2


def kernel(
    ncl, nri,
    ten, live, sizes, occ, vir,
    out,
    nat, fnat, own_t, up_t, c1a, c1b, cmb,
    z0, zp, zm, f0, fp, zn, perm, vmat, omat, occ_f, vir_f, acc, rin, rsend,
    s_nat, r_nat, l_nat, s_up, r_up, s_c1a, r_c1a, s_c1b, r_c1b, s_cmb, r_cmb,
    s_occ, r_occ, s_vir, r_vir, l_den, s_res, r_res,
):
    S = ten.shape[2]
    B = ten.shape[3]
    DR = occ.shape[2]
    NQ = S // 16
    NMC = B // MC
    NK = 3 * NMC
    c = lax.axis_index("pair")
    y = lax.axis_index("ri")

    def cl(d):
        return lax.rem(c + (d + ncl), ncl)

    def rw(d):
        return lax.rem(y + (d + nri), nri)

    def remote(src, dst, ss, rs, dc, dy):
        return pltpu.make_async_remote_copy(
            src_ref=src, dst_ref=dst, send_sem=ss, recv_sem=rs,
            device_id=(cl(dc), rw(dy)), device_id_type=MESH,
        )

    barrier = pltpu.get_barrier_semaphore()
    others = [(dc, dy) for dc in (-1, 0, 1) for dy in range(nri) if (dc, dy) != (0, 0)]
    for dc, dy in others:
        pl.semaphore_signal(barrier, inc=1, device_id=(cl(dc), rw(dy)), device_id_type=MESH)

    nat_copies = [
        pltpu.make_async_copy(ten.at[0, s], nat.at[s], l_nat.at[s]) for s in range(3)
    ]
    for cp in nat_copies:
        cp.start()
    my_rows = pl.ds(pl.multiple_of(y * DR, DR), DR)
    den_copies = [
        pltpu.make_async_copy(occ.at[0], occ_f.at[:, my_rows], l_den.at[0]),
        pltpu.make_async_copy(vir.at[0], vir_f.at[1, :, my_rows], l_den.at[1]),
    ]
    for cp in den_copies:
        cp.start()
    row = lax.broadcasted_iota(jnp.int32, (256, 256), 0)
    col = lax.broadcasted_iota(jnp.int32, (256, 256), 1)
    perm[...] = jnp.where(
        (row // 16 == col % 16) & (row % 16 == col // 16), 1.0, 0.0
    ).astype(BF)
    for r in range(acc.shape[0]):
        acc[r] = jnp.zeros(acc.shape[1:], F32)
    def relay(s, mc):
        for mb in range(MC // 16):
            m0 = pl.multiple_of(mc * MC + mb * 16, 16)
            for j in range(NQ):
                x = nat[s, pl.ds(16 * j, 16), pl.ds(m0, 16), :].reshape(256, B)
                t = jnp.dot(perm[...], x, preferred_element_type=F32).astype(BF)
                own_t[s, pl.ds(m0, 16), pl.ds(16 * j, 16), :] = t.reshape(16, 16, B)

    nat_copies[0].wait()

    @pl.loop(0, NMC)
    def _(mc):
        relay(0, mc)

    pl.semaphore_wait(barrier, len(others))

    first_sends = []
    for dy in range(1, nri):
        first_sends.append(
            remote(occ.at[0], occ_f.at[:, my_rows], s_occ.at[dy - 1], r_occ.at[dy - 1], 0, dy)
        )
        first_sends.append(
            remote(vir.at[0], vir_f.at[1, :, my_rows], s_vir.at[dy - 1], r_vir.at[dy - 1], 0, dy)
        )
    for cp in first_sends:
        cp.start()

    def nat_send(j):
        n = S // NK
        q = pl.ds(pl.multiple_of(n * j, n), n)
        return remote(ten.at[0, :, q], fnat.at[:, q], s_nat.at[j], r_nat.at[j], 0, 1)

    @pl.loop(0, NK)
    def _(j):
        nat_send(j).start()

    def part(k):
        return lax.div(k, NMC), pl.ds(pl.multiple_of(lax.rem(k, NMC) * MC, MC), MC)

    def up_send(k):
        s, m = part(k)
        return remote(own_t.at[s, m], up_t.at[s, m], s_up.at[k], r_up.at[k], 0, -1)

    def c1a_send(k):
        s, m = part(k)
        return remote(own_t.at[s, m], c1a.at[s, m], s_c1a.at[k], r_c1a.at[k], -1, 0)

    def c1b_send(k):
        s, m = part(k)
        return remote(up_t.at[s, m], c1b.at[s, m], s_c1b.at[k], r_c1b.at[k], -1, 0)

    def cmb_send(k):
        s, m = part(k)
        return remote(up_t.at[s, m], cmb.at[s, m], s_cmb.at[k], r_cmb.at[k], 1, 0)

    @pl.loop(0, NMC)
    def _(k):
        up_send(k).start()

    for cp in den_copies:
        cp.wait()
    for cp in first_sends:
        cp.wait_recv()
    next_sends = [
        remote(vir_f.at[1], vir_f.at[1 - dc], s_vir.at[nri + dc], r_vir.at[nri + dc], dc, 0)
        for dc in (-1, 1)
    ]
    for cp in next_sends:
        cp.start()

    @pl.loop(0, NMC)
    def _(k):
        c1a_send(k).start()

    for s in (1, 2):
        nat_copies[s].wait()

        @pl.loop(0, NMC)
        def _(mc, s=s):
            relay(s, mc)
            up_send(s * NMC + mc).start()
            c1a_send(s * NMC + mc).start()

    for cp in next_sends:
        cp.wait_recv()
    size = {d: sizes[cl(d)] for d in range(-2, 3)}
    ri_ = lax.broadcasted_iota(jnp.int32, (B, B), 0)
    ci_ = lax.broadcasted_iota(jnp.int32, (B, B), 1)
    for u in (-1, 0, 1):
        on = live[u + 1, c].astype(F32)
        for t in (u - 1, u, u + 1):
            keep = jnp.where((ri_ < size[u]) & (ci_ < size[t]), on, 0.0)
            v = vir_f[u + 1, t - u + 1].astype(F32) * keep
            vmat[pl.ds((u + 1) * B, B), pl.ds((t + 2) * B, B)] = v.astype(BF)
    zero = jnp.zeros((B, B), BF)
    for u in (-1, 0, 1):
        for t in range(-2, 3):
            if abs(t - u) > 1:
                vmat[pl.ds((u + 1) * B, B), pl.ds((t + 2) * B, B)] = zero
    for g in (-1, 0, 1):
        o = occ_f[g + 1].astype(F32)
        o = jnp.where((ri_ < size[0]) & (ci_ < size[g]), o, 0.0)
        omat[g + 1] = o.T.astype(BF)

    def apply(src, q0, first, count, gs):
        @pl.loop(first, first + count)
        def _(i):
            qs = [q0 + 2 * i, q0 + 2 * i + 1]
            x = jnp.concatenate(
                [jnp.concatenate([src[u, q] for u in range(3)], axis=1) for q in qs], axis=0
            )
            lo = jnp.dot(
                x[:, : 2 * B], vmat[pl.ds(0, 2 * B), pl.ds(0, 2 * B)],
                preferred_element_type=F32,
            ).astype(BF)
            mid = jnp.dot(
                x, vmat[:, pl.ds(2 * B, B)], preferred_element_type=F32
            ).astype(BF)
            hi = jnp.dot(
                x[:, B:], vmat[pl.ds(B, 2 * B), pl.ds(3 * B, 2 * B)],
                preferred_element_type=F32,
            ).astype(BF)
            yy = jnp.concatenate([lo, mid, hi], axis=1)
            for n in range(2):
                rows = yy[n * B : (n + 1) * B]
                for slot, g in enumerate(gs):
                    zn[slot, 2 * i + n] = jnp.dot(
                        omat[g + 1], rows[:, (g + 1) * B : (g + 4) * B],
                        preferred_element_type=F32,
                    ).astype(BF)

    def lead(q0, dests):
        @pl.loop(0, B // 16)
        def _(mb):
            m0 = pl.multiple_of(mb * 16, 16)
            for slot, dst in enumerate(dests):
                x = zn[slot, :, pl.ds(m0, 16), :].reshape(256, 3 * B)
                t = jnp.dot(perm[...], x, preferred_element_type=F32).astype(BF)
                for s in range(3):
                    dst[s, pl.ds(m0, 16), pl.ds(q0, 16), :] = t[
                        :, s * B : (s + 1) * B
                    ].reshape(16, 16, B)

    @pl.loop(0, NQ)
    def _(j):
        q0 = pl.multiple_of(16 * j, 16)
        apply(nat, q0, 0, 8, (-1, 0, 1))
        lead(q0, (zm, z0, zp))

    for cp in first_sends + next_sends:
        cp.wait_send()

    def gram(r, left, right, dc, s, m0, count, lo=0, hi=None):
        hi = S if hi is None else hi
        total = jnp.zeros((S, hi - lo), F32)
        for i in range(0, count, 2):
            a = jnp.concatenate([left[s, m0 + i], left[s, m0 + i + 1]], axis=1)
            b = jnp.concatenate(
                [right[s, m0 + i, pl.ds(lo, hi - lo)], right[s, m0 + i + 1, pl.ds(lo, hi - lo)]],
                axis=1,
            )
            total += lax.dot_general(a, b, NT, preferred_element_type=F32)
        acc[r, :, pl.ds(lo, hi - lo)] += total * live[s, cl(dc)].astype(F32)

    def chunk(r, left, right, dc, k):
        gram(r, left, right, dc, lax.div(k, NMC), lax.rem(k, NMC) * MC, MC)

    def halfway(r, left, right, dc, h, lo=0, hi=None):
        gram(r, left, right, dc, lax.div(h, 2), lax.rem(h, 2) * (B // 2), B // 2, lo, hi)

    def late(k):
        c1b_send(k).wait_recv()
        chunk(4, c1b, zp, 1, k)
        cmb_send(k).wait_recv()
        chunk(6, cmb, zm, -1, k)
        c1b_send(k).wait_send()
        cmb_send(k).wait_send()

    cpj = NK // NQ
    PQ = 8 // cpj
    CUT = S - 16

    def arrivals(first, last):
        @pl.loop(first, last)
        def _(k):
            up_send(k).wait_recv()
            c1b_send(k).start()
            cmb_send(k).start()
            chunk(0, own_t, z0, 0, k)
            chunk(1, up_t, z0, 0, k)
            c1a_send(k).wait_recv()
            chunk(3, c1a, zp, 1, k)
            up_send(k).wait_send()
            c1a_send(k).wait_send()

            @pl.when(k >= LAG)
            def _():
                late(k - LAG)

            q0 = pl.multiple_of(lax.div(k, cpj) * 16, 16)
            i = lax.rem(k, cpj)
            nat_send(k).wait_recv()
            apply(fnat, q0, i * PQ, PQ, (0, 1))
            nat_send(k).wait_send()

            @pl.when(i == cpj - 1)
            def _():
                lead(q0, (f0, fp))

    arrivals(0, (NQ - 1) * cpj)

    EARLY = 6 * (NQ - 1) // NQ - 1
    if CUT:

        @pl.loop(0, EARLY)
        def _(h):
            halfway(2, up_t, f0, 0, h, 0, CUT)
            halfway(5, c1b, fp, 1, h, 0, CUT)

    arrivals((NQ - 1) * cpj, NK)
    slots = [
        (1, False), (2, False), (3, False), (4, False), (5, False), (5, True), (6, False)
    ]
    sends = []

    def deliver(first, count, dc, dy):
        for i in range(first, first + count):
            r, flip = slots[i]
            v = acc[r]
            rsend[i, :, pl.ds(0, S)] = v.T if flip else v
        run = pl.ds(first, count)
        cp = remote(
            rsend.at[run], rin.at[run], s_res.at[len(sends)], r_res.at[len(sends)], dc, dy
        )
        cp.start()
        sends.append(cp)

    deliver(0, 1, 0, 1)
    deliver(2, 1, 1, 0)
    @pl.loop(0, EARLY)
    def _(h):
        halfway(2, up_t, f0, 0, h, CUT, S)
        halfway(5, c1b, fp, 1, h, CUT, S)

    @pl.loop(EARLY, 5)
    def _(h):
        halfway(2, up_t, f0, 0, h)
        halfway(5, c1b, fp, 1, h)

    halfway(2, up_t, f0, 0, 5)
    deliver(1, 1, 0, 1)

    @pl.loop(NK - LAG, NK)
    def _(k):
        late(k)

    deliver(6, 1, -1, 1)
    halfway(5, c1b, fp, 1, 5)
    deliver(3, 2, 1, 1)
    deliver(5, 1, 0, -1)

    blocks = {
        (0, 0): acc[0],
        (0, 1): acc[1].T,
        (1, 0): acc[3].T,
        (1, 1): acc[4].T,
        (-1, 1): acc[6].T,
    }
    landed = [(0, 3), (0, 2), (-1, 0), (-1, 3), (-1, 2), (1, 2), (1, 3)]
    for cp in sends:
        cp.wait_recv()
    for i, (g, dy) in enumerate(landed):
        blocks[g, dy] = rin[i, :, pl.ds(0, S)]
    for yy in range(nri):

        @pl.when(y == yy)
        def _(yy=yy):
            for g in (-1, 0, 1):
                out[g + 1] = jnp.concatenate(
                    [blocks[g, (py - yy) % nri] for py in range(nri)], axis=1
                )

    for cp in sends:
        cp.wait_send()


def per_device(ncl, nri, tensor, live, sizes, occ, vir):
    S, B = tensor.shape[2], tensor.shape[3]
    NQ, NK = S // 16, 3 * (B // MC)
    block = pltpu.VMEM((3, B, S, B), BF)
    dma = lambda n: pltpu.SemaphoreType.DMA((n,))
    n_vir = nri + 2
    any_, smem = pl.BlockSpec(memory_space=pl.ANY), pl.BlockSpec(memory_space=pltpu.SMEM)
    result = pl.pallas_call(
        functools.partial(kernel, ncl, nri),
        out_shape=jax.ShapeDtypeStruct((3, S, nri * S), F32),
        in_specs=[any_, smem, smem, any_, any_],
        out_specs=pl.BlockSpec(memory_space=pltpu.VMEM),
        scratch_shapes=[
            pltpu.VMEM((3, S, B, B), BF), pltpu.VMEM((3, S, B, B), BF),
            block, block, block, block, block,
            block, block, block, block, block,
            pltpu.VMEM((3, 16, B, 3 * B), BF),
            pltpu.VMEM((256, 256), BF),
            pltpu.VMEM((3 * B, 5 * B), BF),
            pltpu.VMEM((3, B, B), BF),
            pltpu.VMEM((3, B, B), BF),
            pltpu.VMEM((3, 3, B, B), BF),
            pltpu.VMEM((7, S, S), F32),
            pltpu.VMEM((7, S, 128), F32),
            pltpu.VMEM((7, S, 128), F32),
            dma(NK), dma(NK), dma(3),
            dma(NK), dma(NK), dma(NK), dma(NK), dma(NK), dma(NK), dma(NK), dma(NK),
            dma(nri - 1), dma(nri - 1), dma(n_vir), dma(n_vir), dma(2),
            dma(6), dma(6),
        ],
        compiler_params=pltpu.CompilerParams(
            collective_id=0, has_side_effects=True, vmem_limit_bytes=63 * 1024 * 1024
        ),
        name="polar",
    )(tensor, live.T, sizes, occ, vir)
    return jnp.swapaxes(result, 1, 2)[None]


def solution(mesh):
    ncl, nri = mesh.shape["pair"], mesh.shape["ri"]
    in_specs = (
        P("pair", None, "ri", None, None),
        P(),
        P(),
        P("pair", None, "ri", None),
        P("pair", None, "ri", None),
    )
    return jax.shard_map(
        functools.partial(per_device, ncl, nri),
        mesh=mesh,
        in_specs=in_specs,
        out_specs=P("pair", None, None, "ri"),
        check_vma=False,
    )
```

```python
import functools

import jax
import jax.numpy as jnp
from jax import lax
from jax.experimental import pallas as pl
from jax.experimental.pallas import tpu as pltpu
from jax.sharding import PartitionSpec as P

MESH = pl.DeviceIdType.MESH
BF = jnp.bfloat16
F32 = jnp.float32
NT = (((1,), (1,)), ((), ()))
MC = 32
SUB = 4


def kernel(
    ncl, nri,
    ten, live, sizes, occ, vir,
    out,
    nat, fnat, own_t, up_t, c1a, c1b, cmb,
    z0, zp, zm, f0, fp, zn, perm, vmat, omat, occ_f, vir_f, acc, rin, rsend,
    s_nat, r_nat, l_nat, s_up, r_up, s_c1a, r_c1a, s_c1b, r_c1b, s_cmb, r_cmb,
    s_occ, r_occ, s_vir, r_vir, l_den, s_res, r_res,
):
    S = ten.shape[2]
    B = ten.shape[3]
    DR = occ.shape[2]
    NQ = S // 16
    NMC = B // MC
    NK = 3 * NMC
    c = lax.axis_index("pair")
    y = lax.axis_index("ri")

    def cl(d):
        return lax.rem(c + (d + ncl), ncl)

    def rw(d):
        return lax.rem(y + (d + nri), nri)

    def remote(src, dst, ss, rs, dc, dy):
        return pltpu.make_async_remote_copy(
            src_ref=src, dst_ref=dst, send_sem=ss, recv_sem=rs,
            device_id=(cl(dc), rw(dy)), device_id_type=MESH,
        )

    barrier = pltpu.get_barrier_semaphore()
    others = [
        (dc, dy)
        for dc in (-1, 0, 1)
        for dy in range(nri)
        if (dc, dy) != (0, 0) and (dc == 0 or dy in (0, 1, nri - 1))
    ]
    for dc, dy in others:
        pl.semaphore_signal(barrier, inc=1, device_id=(cl(dc), rw(dy)), device_id_type=MESH)

    nat_copies = [
        pltpu.make_async_copy(ten.at[0, s], nat.at[s], l_nat.at[s]) for s in range(3)
    ]
    for cp in nat_copies:
        cp.start()
    my_rows = pl.ds(pl.multiple_of(y * DR, DR), DR)
    den_copies = [
        pltpu.make_async_copy(occ.at[0], occ_f.at[:, my_rows], l_den.at[0]),
        pltpu.make_async_copy(vir.at[0], vir_f.at[1, :, my_rows], l_den.at[1]),
    ]
    for cp in den_copies:
        cp.start()
    row = lax.broadcasted_iota(jnp.int32, (256, 256), 0)
    col = lax.broadcasted_iota(jnp.int32, (256, 256), 1)
    perm[...] = jnp.where(
        (row // 16 == col % 16) & (row % 16 == col // 16), 1.0, 0.0
    ).astype(BF)
    for r in range(acc.shape[0]):
        acc[r] = jnp.zeros(acc.shape[1:], F32)
    def relay(s, mc):
        for mb in range(MC // 16):
            m0 = pl.multiple_of(mc * MC + mb * 16, 16)
            for j in range(NQ):
                x = nat[s, pl.ds(16 * j, 16), pl.ds(m0, 16), :].reshape(256, B)
                t = jnp.dot(perm[...], x, preferred_element_type=F32).astype(BF)
                own_t[s, pl.ds(m0, 16), pl.ds(16 * j, 16), :] = t.reshape(16, 16, B)

    nat_copies[0].wait()

    @pl.loop(0, NMC)
    def _(mc):
        relay(0, mc)

    pl.semaphore_wait(barrier, len(others))

    first_sends = []
    for dy in range(1, nri):
        first_sends.append(
            remote(occ.at[0], occ_f.at[:, my_rows], s_occ.at[dy - 1], r_occ.at[dy - 1], 0, dy)
        )
        first_sends.append(
            remote(vir.at[0], vir_f.at[1, :, my_rows], s_vir.at[dy - 1], r_vir.at[dy - 1], 0, dy)
        )
    for cp in first_sends:
        cp.start()

    def nat_send(j):
        n = S // NK
        q = pl.ds(pl.multiple_of(n * j, n), n)
        return remote(ten.at[0, :, q], fnat.at[:, q], s_nat.at[j], r_nat.at[j], 0, 1)

    @pl.loop(0, NK)
    def _(j):
        nat_send(j).start()

    LAST = NK - 1

    def part(k):
        if isinstance(k, int) and k >= LAST:
            n = MC // SUB
            return 2, pl.ds(B - MC + (k - LAST) * n, n)
        return lax.div(k, NMC), pl.ds(pl.multiple_of(lax.rem(k, NMC) * MC, MC), MC)

    def up_send(k):
        s, m = part(k)
        return remote(own_t.at[s, m], up_t.at[s, m], s_up.at[k], r_up.at[k], 0, -1)

    def c1a_send(k):
        s, m = part(k)
        return remote(own_t.at[s, m], c1a.at[s, m], s_c1a.at[k], r_c1a.at[k], -1, 0)

    def c1b_send(k):
        s, m = part(k)
        return remote(up_t.at[s, m], c1b.at[s, m], s_c1b.at[k], r_c1b.at[k], -1, 0)

    def cmb_send(k):
        s, m = part(k)
        return remote(up_t.at[s, m], cmb.at[s, m], s_cmb.at[k], r_cmb.at[k], 1, 0)

    @pl.loop(0, NMC)
    def _(k):
        up_send(k).start()

    for cp in den_copies:
        cp.wait()
    for cp in first_sends:
        cp.wait_recv()
    next_sends = [
        remote(vir_f.at[1], vir_f.at[1 - dc], s_vir.at[nri + dc], r_vir.at[nri + dc], dc, 0)
        for dc in (-1, 1)
    ]
    for cp in next_sends:
        cp.start()

    @pl.loop(0, NMC)
    def _(k):
        c1a_send(k).start()

    for s in (1, 2):
        nat_copies[s].wait()

        @pl.loop(0, NMC)
        def _(mc, s=s):
            relay(s, mc)
            k = s * NMC + mc

            @pl.when(k < LAST)
            def _():
                up_send(k).start()
                c1a_send(k).start()

    for i in range(SUB):
        up_send(LAST + i).start()
        c1a_send(LAST + i).start()

    for cp in next_sends:
        cp.wait_recv()
    size = {d: sizes[cl(d)] for d in range(-2, 3)}
    ri_ = lax.broadcasted_iota(jnp.int32, (B, B), 0)
    ci_ = lax.broadcasted_iota(jnp.int32, (B, B), 1)
    for u in (-1, 0, 1):
        on = live[u + 1, c].astype(F32)
        for t in (u - 1, u, u + 1):
            keep = jnp.where((ri_ < size[u]) & (ci_ < size[t]), on, 0.0)
            v = vir_f[u + 1, t - u + 1].astype(F32) * keep
            vmat[pl.ds((u + 1) * B, B), pl.ds((t + 2) * B, B)] = v.astype(BF)
    zero = jnp.zeros((B, B), BF)
    for u in (-1, 0, 1):
        for t in range(-2, 3):
            if abs(t - u) > 1:
                vmat[pl.ds((u + 1) * B, B), pl.ds((t + 2) * B, B)] = zero
    for g in (-1, 0, 1):
        o = occ_f[g + 1].astype(F32)
        o = jnp.where((ri_ < size[0]) & (ci_ < size[g]), o, 0.0)
        omat[g + 1] = o.T.astype(BF)

    def apply(src, q0, first, count, gs):
        @pl.loop(first, first + count)
        def _(i):
            qs = [q0 + 2 * i, q0 + 2 * i + 1]
            x = jnp.concatenate(
                [jnp.concatenate([src[u, q] for u in range(3)], axis=1) for q in qs], axis=0
            )
            lo = jnp.dot(
                x[:, : 2 * B], vmat[pl.ds(0, 2 * B), pl.ds(0, 2 * B)],
                preferred_element_type=F32,
            ).astype(BF)
            mid = jnp.dot(
                x, vmat[:, pl.ds(2 * B, B)], preferred_element_type=F32
            ).astype(BF)
            hi = jnp.dot(
                x[:, B:], vmat[pl.ds(B, 2 * B), pl.ds(3 * B, 2 * B)],
                preferred_element_type=F32,
            ).astype(BF)
            yy = jnp.concatenate([lo, mid, hi], axis=1)
            for n in range(2):
                rows = yy[n * B : (n + 1) * B]
                for slot, g in enumerate(gs):
                    zn[slot, 2 * i + n] = jnp.dot(
                        omat[g + 1], rows[:, (g + 1) * B : (g + 4) * B],
                        preferred_element_type=F32,
                    ).astype(BF)

    def lead(q0, dests):
        @pl.loop(0, B // 16)
        def _(mb):
            m0 = pl.multiple_of(mb * 16, 16)
            for slot, dst in enumerate(dests):
                x = zn[slot, :, pl.ds(m0, 16), :].reshape(256, 3 * B)
                t = jnp.dot(perm[...], x, preferred_element_type=F32).astype(BF)
                for s in range(3):
                    dst[s, pl.ds(m0, 16), pl.ds(q0, 16), :] = t[
                        :, s * B : (s + 1) * B
                    ].reshape(16, 16, B)

    @pl.loop(0, NQ)
    def _(j):
        q0 = pl.multiple_of(16 * j, 16)
        apply(nat, q0, 0, 8, (-1, 0, 1))
        lead(q0, (zm, z0, zp))

    for cp in first_sends + next_sends:
        cp.wait_send()

    def gram(r, left, right, dc, s, m0, count):
        total = jnp.zeros((S, S), F32)
        for i in range(0, count, 2):
            a = jnp.concatenate([left[s, m0 + i], left[s, m0 + i + 1]], axis=1)
            b = jnp.concatenate([right[s, m0 + i], right[s, m0 + i + 1]], axis=1)
            total += lax.dot_general(a, b, NT, preferred_element_type=F32)
        acc[r] += total * live[s, cl(dc)].astype(F32)

    def chunk(r, left, right, dc, k):
        gram(r, left, right, dc, lax.div(k, NMC), lax.rem(k, NMC) * MC, MC)

    def halfway(r, left, right, dc, h):
        gram(r, left, right, dc, lax.div(h, 2), lax.rem(h, 2) * (B // 2), B // 2)

    def late(k):
        c1b_send(k).wait_recv()
        cmb_send(k).wait_recv()
        chunk(4, c1b, zp, 1, k)
        chunk(6, cmb, zm, -1, k)
        c1b_send(k).wait_send()
        cmb_send(k).wait_send()

    FROM = LAST - 4
    cpj = NK // NQ
    PQ = 8 // cpj

    def piece(k):
        q0 = pl.multiple_of(lax.div(k, cpj) * 16, 16)
        i = lax.rem(k, cpj)
        nat_send(k).wait_recv()
        apply(fnat, q0, i * PQ, PQ, (0, 1))

        @pl.when(i == cpj - 1)
        def _():
            lead(q0, (f0, fp))

        nat_send(k).wait_send()

    @pl.loop(0, LAST)
    def _(k):
        c1a_send(k).wait_recv()
        chunk(3, c1a, zp, 1, k)
        c1a_send(k).wait_send()

        @pl.when(k >= FROM)
        def _():
            late(2 * (k - FROM))
            late(2 * (k - FROM) + 1)

        up_send(k).wait_recv()
        c1b_send(k).start()
        cmb_send(k).start()
        chunk(0, own_t, z0, 0, k)
        chunk(1, up_t, z0, 0, k)
        up_send(k).wait_send()
        piece(k)

    for i in range(SUB):
        c1a_send(LAST + i).wait_recv()
    chunk(3, c1a, zp, 1, LAST)
    chunk(0, own_t, z0, 0, LAST)
    late(LAST - 3)
    late(LAST - 2)
    for i in range(SUB):
        up_send(LAST + i).wait_recv()
        c1b_send(LAST + i).start()
        cmb_send(LAST + i).start()
    chunk(1, up_t, z0, 0, LAST)

    slots = [
        (1, False), (2, False), (3, False), (4, False), (5, False), (5, True), (6, False)
    ]
    sends = []

    def deliver(first, count, dc, dy):
        for i in range(first, first + count):
            r, flip = slots[i]
            v = acc[r]
            rsend[i, :, pl.ds(0, S)] = v.T if flip else v
        run = pl.ds(first, count)
        cp = remote(
            rsend.at[run], rin.at[run], s_res.at[len(sends)], r_res.at[len(sends)], dc, dy
        )
        cp.start()
        sends.append(cp)

    deliver(2, 1, 1, 0)
    deliver(0, 1, 0, 1)
    piece(LAST)

    @pl.loop(0, 5)
    def _(h):
        halfway(2, up_t, f0, 0, h)
        halfway(5, c1b, fp, 1, h)

    halfway(2, up_t, f0, 0, 5)
    deliver(1, 1, 0, 1)
    late(LAST - 1)
    for i in range(SUB):
        cmb_send(LAST + i).wait_recv()
    chunk(6, cmb, zm, -1, LAST)
    deliver(6, 1, -1, 1)
    for i in range(SUB):
        c1b_send(LAST + i).wait_recv()
    chunk(4, c1b, zp, 1, LAST)
    deliver(3, 1, 1, 1)
    halfway(5, c1b, fp, 1, 5)
    deliver(4, 1, 1, 1)
    deliver(5, 1, 0, -1)
    for i in range(SUB):
        up_send(LAST + i).wait_send()
        c1a_send(LAST + i).wait_send()
        c1b_send(LAST + i).wait_send()
        cmb_send(LAST + i).wait_send()

    blocks = {
        (0, 0): acc[0],
        (0, 1): acc[1].T,
        (1, 0): acc[3].T,
        (1, 1): acc[4].T,
        (-1, 1): acc[6].T,
    }
    landed = [(0, 3), (0, 2), (-1, 0), (-1, 3), (-1, 2), (1, 2), (1, 3)]
    for cp in sends:
        cp.wait_recv()
    for i, (g, dy) in enumerate(landed):
        blocks[g, dy] = rin[i, :, pl.ds(0, S)]
    for yy in range(nri):

        @pl.when(y == yy)
        def _(yy=yy):
            for g in (-1, 0, 1):
                out[g + 1] = jnp.concatenate(
                    [blocks[g, (py - yy) % nri] for py in range(nri)], axis=1
                )

    for cp in sends:
        cp.wait_send()


def per_device(ncl, nri, tensor, live, sizes, occ, vir):
    S, B = tensor.shape[2], tensor.shape[3]
    NQ, NK = S // 16, 3 * (B // MC)
    block = pltpu.VMEM((3, B, S, B), BF)
    dma = lambda n: pltpu.SemaphoreType.DMA((n,))
    n_vir = nri + 2
    any_, smem = pl.BlockSpec(memory_space=pl.ANY), pl.BlockSpec(memory_space=pltpu.SMEM)
    result = pl.pallas_call(
        functools.partial(kernel, ncl, nri),
        out_shape=jax.ShapeDtypeStruct((3, S, nri * S), F32),
        in_specs=[any_, smem, smem, any_, any_],
        out_specs=pl.BlockSpec(memory_space=pltpu.VMEM),
        scratch_shapes=[
            pltpu.VMEM((3, S, B, B), BF), pltpu.VMEM((3, S, B, B), BF),
            block, block, block, block, block,
            block, block, block, block, block,
            pltpu.VMEM((3, 16, B, 3 * B), BF),
            pltpu.VMEM((256, 256), BF),
            pltpu.VMEM((3 * B, 5 * B), BF),
            pltpu.VMEM((3, B, B), BF),
            pltpu.VMEM((3, B, B), BF),
            pltpu.VMEM((3, 3, B, B), BF),
            pltpu.VMEM((7, S, S), F32),
            pltpu.VMEM((7, S, 128), F32),
            pltpu.VMEM((7, S, 128), F32),
            dma(NK), dma(NK), dma(3),
            *[dma(NK - 1 + SUB) for _ in range(8)],
            dma(nri - 1), dma(nri - 1), dma(n_vir), dma(n_vir), dma(2),
            dma(7), dma(7),
        ],
        compiler_params=pltpu.CompilerParams(
            collective_id=0, has_side_effects=True, vmem_limit_bytes=63 * 1024 * 1024
        ),
        name="polar",
    )(tensor, live.T, sizes, occ, vir)
    return jnp.swapaxes(result, 1, 2)[None]


def solution(mesh):
    ncl, nri = mesh.shape["pair"], mesh.shape["ri"]
    in_specs = (
        P("pair", None, "ri", None, None),
        P(),
        P(),
        P("pair", None, "ri", None),
        P("pair", None, "ri", None),
    )
    return jax.shard_map(
        functools.partial(per_device, ncl, nri),
        mesh=mesh,
        in_specs=in_specs,
        out_specs=P("pair", None, None, "ri"),
        check_vma=False,
    )
```

```python
import functools

import jax
import jax.numpy as jnp
from jax import lax
from jax.experimental import pallas as pl
from jax.experimental.pallas import tpu as pltpu
from jax.sharding import PartitionSpec as P

MESH = pl.DeviceIdType.MESH
BF = jnp.bfloat16
F32 = jnp.float32
NT = (((1,), (1,)), ((), ()))
MC = 32
SUB = 2


def kernel(
    ncl, nri,
    ten, live, sizes, occ, vir,
    out,
    nat, fnat, own_t, up_t, c1a, c1b, cmb,
    z0, zp, zm, f0, fp, zn, perm, vmat, omat, occ_f, vir_f, acc, rin, rsend,
    s_nat, r_nat, l_nat, s_up, r_up, s_c1a, r_c1a, s_c1b, r_c1b, s_cmb, r_cmb,
    s_occ, r_occ, s_vir, r_vir, l_den, s_res, r_res,
):
    S = ten.shape[2]
    B = ten.shape[3]
    DR = occ.shape[2]
    NQ = S // 16
    NMC = B // MC
    NK = 3 * NMC
    c = lax.axis_index("pair")
    y = lax.axis_index("ri")

    def cl(d):
        return lax.rem(c + (d + ncl), ncl)

    def rw(d):
        return lax.rem(y + (d + nri), nri)

    def remote(src, dst, ss, rs, dc, dy):
        return pltpu.make_async_remote_copy(
            src_ref=src, dst_ref=dst, send_sem=ss, recv_sem=rs,
            device_id=(cl(dc), rw(dy)), device_id_type=MESH,
        )

    barrier = pltpu.get_barrier_semaphore()
    others = [
        (dc, dy)
        for dc in (-1, 0, 1)
        for dy in range(nri)
        if (dc, dy) != (0, 0) and (dc == 0 or dy in (0, 1, nri - 1))
    ]
    for dc, dy in others:
        pl.semaphore_signal(barrier, inc=1, device_id=(cl(dc), rw(dy)), device_id_type=MESH)

    nat_copies = [
        pltpu.make_async_copy(ten.at[0, s], nat.at[s], l_nat.at[s]) for s in range(3)
    ]
    for cp in nat_copies:
        cp.start()
    my_rows = pl.ds(pl.multiple_of(y * DR, DR), DR)
    den_copies = [
        pltpu.make_async_copy(occ.at[0], occ_f.at[:, my_rows], l_den.at[0]),
        pltpu.make_async_copy(vir.at[0], vir_f.at[1, :, my_rows], l_den.at[1]),
    ]
    for cp in den_copies:
        cp.start()
    row = lax.broadcasted_iota(jnp.int32, (256, 256), 0)
    col = lax.broadcasted_iota(jnp.int32, (256, 256), 1)
    perm[...] = jnp.where(
        (row // 16 == col % 16) & (row % 16 == col // 16), 1.0, 0.0
    ).astype(BF)
    for r in range(acc.shape[0]):
        acc[r] = jnp.zeros(acc.shape[1:], F32)
    def relay(s, mc):
        for mb in range(MC // 16):
            m0 = pl.multiple_of(mc * MC + mb * 16, 16)
            for j in range(NQ):
                x = nat[s, pl.ds(16 * j, 16), pl.ds(m0, 16), :].reshape(256, B)
                t = jnp.dot(perm[...], x, preferred_element_type=F32).astype(BF)
                own_t[s, pl.ds(m0, 16), pl.ds(16 * j, 16), :] = t.reshape(16, 16, B)

    nat_copies[0].wait()

    @pl.loop(0, NMC)
    def _(mc):
        relay(0, mc)

    pl.semaphore_wait(barrier, len(others))

    first_sends = []
    for dy in range(1, nri):
        first_sends.append(
            remote(occ.at[0], occ_f.at[:, my_rows], s_occ.at[dy - 1], r_occ.at[dy - 1], 0, dy)
        )
        first_sends.append(
            remote(vir.at[0], vir_f.at[1, :, my_rows], s_vir.at[dy - 1], r_vir.at[dy - 1], 0, dy)
        )
    for cp in first_sends:
        cp.start()

    def nat_send(j):
        n = S // NK
        q = pl.ds(pl.multiple_of(n * j, n), n)
        return remote(ten.at[0, :, q], fnat.at[:, q], s_nat.at[j], r_nat.at[j], 0, 1)

    @pl.loop(0, NK)
    def _(j):
        nat_send(j).start()

    LAST = NK - 1

    def part(k):
        if isinstance(k, int) and k >= LAST:
            n = MC // SUB
            return 2, pl.ds(B - MC + (k - LAST) * n, n)
        return lax.div(k, NMC), pl.ds(pl.multiple_of(lax.rem(k, NMC) * MC, MC), MC)

    def up_send(k):
        s, m = part(k)
        return remote(own_t.at[s, m], up_t.at[s, m], s_up.at[k], r_up.at[k], 0, -1)

    def c1a_send(k):
        s, m = part(k)
        return remote(own_t.at[s, m], c1a.at[s, m], s_c1a.at[k], r_c1a.at[k], -1, 0)

    def c1b_send(k):
        s, m = part(k)
        return remote(up_t.at[s, m], c1b.at[s, m], s_c1b.at[k], r_c1b.at[k], -1, 0)

    def cmb_send(k):
        s, m = part(k)
        return remote(up_t.at[s, m], cmb.at[s, m], s_cmb.at[k], r_cmb.at[k], 1, 0)

    @pl.loop(0, NMC)
    def _(k):
        up_send(k).start()

    for cp in den_copies:
        cp.wait()
    for cp in first_sends:
        cp.wait_recv()
    next_sends = [
        remote(vir_f.at[1], vir_f.at[1 - dc], s_vir.at[nri + dc], r_vir.at[nri + dc], dc, 0)
        for dc in (-1, 1)
    ]
    for cp in next_sends:
        cp.start()

    @pl.loop(0, NMC)
    def _(k):
        c1a_send(k).start()

    for s in (1, 2):
        nat_copies[s].wait()

        @pl.loop(0, NMC)
        def _(mc, s=s):
            relay(s, mc)
            k = s * NMC + mc

            @pl.when(k < LAST)
            def _():
                up_send(k).start()
                c1a_send(k).start()

    for i in range(SUB):
        up_send(LAST + i).start()
        c1a_send(LAST + i).start()

    for cp in next_sends:
        cp.wait_recv()
    size = {d: sizes[cl(d)] for d in range(-2, 3)}
    ri_ = lax.broadcasted_iota(jnp.int32, (B, B), 0)
    ci_ = lax.broadcasted_iota(jnp.int32, (B, B), 1)
    for u in (-1, 0, 1):
        on = live[u + 1, c].astype(F32)
        for t in (u - 1, u, u + 1):
            keep = jnp.where((ri_ < size[u]) & (ci_ < size[t]), on, 0.0)
            v = vir_f[u + 1, t - u + 1].astype(F32) * keep
            vmat[pl.ds((u + 1) * B, B), pl.ds((t + 2) * B, B)] = v.astype(BF)
    zero = jnp.zeros((B, B), BF)
    for u in (-1, 0, 1):
        for t in range(-2, 3):
            if abs(t - u) > 1:
                vmat[pl.ds((u + 1) * B, B), pl.ds((t + 2) * B, B)] = zero
    for g in (-1, 0, 1):
        o = occ_f[g + 1].astype(F32)
        o = jnp.where((ri_ < size[0]) & (ci_ < size[g]), o, 0.0)
        omat[g + 1] = o.T.astype(BF)

    def apply(src, q0, first, count, gs):
        @pl.loop(first, first + count)
        def _(i):
            qs = [q0 + 2 * i, q0 + 2 * i + 1]
            x = jnp.concatenate(
                [jnp.concatenate([src[u, q] for u in range(3)], axis=1) for q in qs], axis=0
            )
            lo = jnp.dot(
                x[:, : 2 * B], vmat[pl.ds(0, 2 * B), pl.ds(0, 2 * B)],
                preferred_element_type=F32,
            ).astype(BF)
            mid = jnp.dot(
                x, vmat[:, pl.ds(2 * B, B)], preferred_element_type=F32
            ).astype(BF)
            hi = jnp.dot(
                x[:, B:], vmat[pl.ds(B, 2 * B), pl.ds(3 * B, 2 * B)],
                preferred_element_type=F32,
            ).astype(BF)
            yy = jnp.concatenate([lo, mid, hi], axis=1)
            for n in range(2):
                rows = yy[n * B : (n + 1) * B]
                for slot, g in enumerate(gs):
                    zn[slot, 2 * i + n] = jnp.dot(
                        omat[g + 1], rows[:, (g + 1) * B : (g + 4) * B],
                        preferred_element_type=F32,
                    ).astype(BF)

    def lead(q0, dests):
        @pl.loop(0, B // 16)
        def _(mb):
            m0 = pl.multiple_of(mb * 16, 16)
            for slot, dst in enumerate(dests):
                x = zn[slot, :, pl.ds(m0, 16), :].reshape(256, 3 * B)
                t = jnp.dot(perm[...], x, preferred_element_type=F32).astype(BF)
                for s in range(3):
                    dst[s, pl.ds(m0, 16), pl.ds(q0, 16), :] = t[
                        :, s * B : (s + 1) * B
                    ].reshape(16, 16, B)

    @pl.loop(0, NQ)
    def _(j):
        q0 = pl.multiple_of(16 * j, 16)
        apply(nat, q0, 0, 8, (-1, 0, 1))
        lead(q0, (zm, z0, zp))

    for cp in first_sends + next_sends:
        cp.wait_send()

    def gram(r, left, right, dc, s, m0, count):
        total = jnp.zeros((S, S), F32)
        for i in range(0, count, 2):
            a = jnp.concatenate([left[s, m0 + i], left[s, m0 + i + 1]], axis=1)
            b = jnp.concatenate([right[s, m0 + i], right[s, m0 + i + 1]], axis=1)
            total += lax.dot_general(a, b, NT, preferred_element_type=F32)
        acc[r] += total * live[s, cl(dc)].astype(F32)

    def chunk(r, left, right, dc, k):
        gram(r, left, right, dc, lax.div(k, NMC), lax.rem(k, NMC) * MC, MC)

    def halfway(r, left, right, dc, h):
        gram(r, left, right, dc, lax.div(h, 2), lax.rem(h, 2) * (B // 2), B // 2)

    def late(k):
        c1b_send(k).wait_recv()
        cmb_send(k).wait_recv()
        chunk(4, c1b, zp, 1, k)
        chunk(6, cmb, zm, -1, k)
        c1b_send(k).wait_send()
        cmb_send(k).wait_send()

    FROM = LAST - 4
    cpj = NK // NQ
    PQ = 8 // cpj

    def piece(k):
        q0 = pl.multiple_of(lax.div(k, cpj) * 16, 16)
        i = lax.rem(k, cpj)
        nat_send(k).wait_recv()
        apply(fnat, q0, i * PQ, PQ, (0, 1))

        @pl.when(i == cpj - 1)
        def _():
            lead(q0, (f0, fp))

        nat_send(k).wait_send()

    @pl.loop(0, LAST)
    def _(k):
        c1a_send(k).wait_recv()
        chunk(3, c1a, zp, 1, k)
        c1a_send(k).wait_send()

        @pl.when(k >= FROM)
        def _():
            late(2 * (k - FROM))
            late(2 * (k - FROM) + 1)

        up_send(k).wait_recv()
        c1b_send(k).start()
        cmb_send(k).start()
        chunk(0, own_t, z0, 0, k)
        chunk(1, up_t, z0, 0, k)
        up_send(k).wait_send()
        piece(k)

    for i in range(SUB):
        c1a_send(LAST + i).wait_recv()
    chunk(3, c1a, zp, 1, LAST)
    chunk(0, own_t, z0, 0, LAST)
    late(LAST - 3)
    late(LAST - 2)
    for i in range(SUB):
        up_send(LAST + i).wait_recv()
        c1b_send(LAST + i).start()
        cmb_send(LAST + i).start()
    chunk(1, up_t, z0, 0, LAST)

    slots = [
        (1, False), (2, False), (3, False), (4, False), (5, False), (5, True), (6, False)
    ]
    sends = []

    def deliver(first, count, dc, dy):
        for i in range(first, first + count):
            r, flip = slots[i]
            v = acc[r]
            rsend[i, :, pl.ds(0, S)] = v.T if flip else v
        run = pl.ds(first, count)
        cp = remote(
            rsend.at[run], rin.at[run], s_res.at[len(sends)], r_res.at[len(sends)], dc, dy
        )
        cp.start()
        sends.append(cp)

    deliver(2, 1, 1, 0)
    deliver(0, 1, 0, 1)
    piece(LAST)

    @pl.loop(0, 5)
    def _(h):
        halfway(2, up_t, f0, 0, h)
        halfway(5, c1b, fp, 1, h)

    halfway(2, up_t, f0, 0, 5)
    deliver(1, 1, 0, 1)
    late(LAST - 1)
    for i in range(SUB):
        cmb_send(LAST + i).wait_recv()
    chunk(6, cmb, zm, -1, LAST)
    deliver(6, 1, -1, 1)
    for i in range(SUB):
        c1b_send(LAST + i).wait_recv()
    chunk(4, c1b, zp, 1, LAST)
    deliver(3, 1, 1, 1)
    halfway(5, c1b, fp, 1, 5)
    deliver(4, 1, 1, 1)
    deliver(5, 1, 0, -1)
    for i in range(SUB):
        up_send(LAST + i).wait_send()
        c1a_send(LAST + i).wait_send()
        c1b_send(LAST + i).wait_send()
        cmb_send(LAST + i).wait_send()

    blocks = {
        (0, 0): acc[0],
        (0, 1): acc[1].T,
        (1, 0): acc[3].T,
        (1, 1): acc[4].T,
        (-1, 1): acc[6].T,
    }
    landed = [(0, 3), (0, 2), (-1, 0), (-1, 3), (-1, 2), (1, 2), (1, 3)]
    for cp in sends:
        cp.wait_recv()
    for i, (g, dy) in enumerate(landed):
        blocks[g, dy] = rin[i, :, pl.ds(0, S)]
    for yy in range(nri):

        @pl.when(y == yy)
        def _(yy=yy):
            for g in (-1, 0, 1):
                out[g + 1] = jnp.concatenate(
                    [blocks[g, (py - yy) % nri] for py in range(nri)], axis=1
                )

    for cp in sends:
        cp.wait_send()


def per_device(ncl, nri, tensor, live, sizes, occ, vir):
    S, B = tensor.shape[2], tensor.shape[3]
    NQ, NK = S // 16, 3 * (B // MC)
    block = pltpu.VMEM((3, B, S, B), BF)
    dma = lambda n: pltpu.SemaphoreType.DMA((n,))
    n_vir = nri + 2
    any_, smem = pl.BlockSpec(memory_space=pl.ANY), pl.BlockSpec(memory_space=pltpu.SMEM)
    result = pl.pallas_call(
        functools.partial(kernel, ncl, nri),
        out_shape=jax.ShapeDtypeStruct((3, S, nri * S), F32),
        in_specs=[any_, smem, smem, any_, any_],
        out_specs=pl.BlockSpec(memory_space=pltpu.VMEM),
        scratch_shapes=[
            pltpu.VMEM((3, S, B, B), BF), pltpu.VMEM((3, S, B, B), BF),
            block, block, block, block, block,
            block, block, block, block, block,
            pltpu.VMEM((3, 16, B, 3 * B), BF),
            pltpu.VMEM((256, 256), BF),
            pltpu.VMEM((3 * B, 5 * B), BF),
            pltpu.VMEM((3, B, B), BF),
            pltpu.VMEM((3, B, B), BF),
            pltpu.VMEM((3, 3, B, B), BF),
            pltpu.VMEM((7, S, S), F32),
            pltpu.VMEM((7, S, 128), F32),
            pltpu.VMEM((7, S, 128), F32),
            dma(NK), dma(NK), dma(3),
            *[dma(NK - 1 + SUB) for _ in range(8)],
            dma(nri - 1), dma(nri - 1), dma(n_vir), dma(n_vir), dma(2),
            dma(7), dma(7),
        ],
        compiler_params=pltpu.CompilerParams(
            collective_id=0, has_side_effects=True, vmem_limit_bytes=63 * 1024 * 1024
        ),
        name="polar",
    )(tensor, live.T, sizes, occ, vir)
    return jnp.swapaxes(result, 1, 2)[None]


def solution(mesh):
    ncl, nri = mesh.shape["pair"], mesh.shape["ri"]
    in_specs = (
        P("pair", None, "ri", None, None),
        P(),
        P(),
        P("pair", None, "ri", None),
        P("pair", None, "ri", None),
    )
    return jax.shard_map(
        functools.partial(per_device, ncl, nri),
        mesh=mesh,
        in_specs=in_specs,
        out_specs=P("pair", None, None, "ri"),
        check_vma=False,
    )
```
